512 devices in a mesh: replica: 4 (over x), fsdp: 16 (over z), tensor: 8 (over y, core).
Axes of the slice: x: 4, y: 4, z: 16, core: 2. Of those that a mesh axis runs over, the one named last changes fastest.
Arguments:
- momentum: float32 [4, 4096, 14336], P('replica', 'fsdp', 'tensor'), may hold values from -600 to 600
- gradient: bfloat16 [4, 4096, 14336], P('replica', 'fsdp', 'tensor'), may hold values from -300 to 300
- right_in: float32 [14336, 256], P(('tensor', 'fsdp')), may hold values from -6 to 6
Outputs:
- left_factor: float32 [4096, 256], P('fsdp')
- right_factor: float32 [14336, 256], P(('tensor', 'fsdp'))
- new_momentum: float32 [4, 4096, 14336], P('replica', 'fsdp', 'tensor')
The draws below stay inside these ranges and needn't reach their ends.
All inputs are finite; a program needn't handle non-finite values.
Results may differ from the reference program's by a relative error of at most 0.0003.
Values sent between devices are 32-bit elements; how exact they have to be, the bound alone decides.
No kernel may reach another device: no remote copies, remote signals or barrier semaphores. Data moves between devices by JAX's collectives and lax.ppermute only.
A program may use at most 64 MiB of HBM per device.

```python
import math
import jax
import jax.numpy as jnp
from jax import lax

RANK = 256
REPLICAS = 4
ROWS = 4096
COLS = 14336


def scales(key, count, spread):
    levels = jnp.exp(jax.random.uniform(key, (count,), jnp.float32, -spread, spread))
    rising = jnp.sqrt(1.0 + 2.0 * jnp.arange(count, dtype=jnp.float32) / count)
    return levels * rising


def column_basis(key):
    basis_key = jax.random.fold_in(key, 97)
    return jnp.clip(jax.random.normal(basis_key, (COLS, RANK), jnp.float32), -4.0, 4.0)


def draw_momentum(key, part):
    basis = column_basis(key)
    key = jax.random.fold_in(key, 11)
    key_noise, key_rows, key_cols, key_left = jax.random.split(key, 4)
    left_part = jnp.clip(jax.random.normal(key_left, (ROWS, RANK), jnp.float32), -4.0, 4.0)
    shared = jnp.dot(left_part, basis.T, precision=lax.Precision.HIGHEST) * RANK ** (-0.5)
    shared = jnp.clip(shared, -4.0, 4.0)
    noise = jnp.clip(jax.random.normal(key_noise, (REPLICAS, ROWS, COLS), jnp.float32), -4.0, 4.0)
    row_scale = scales(key_rows, ROWS, 1.1513)
    col_scale = scales(key_cols, COLS, 1.1513)
    mixed = 2.5 * shared[None, :, :] + noise
    return mixed * row_scale[None, :, None] * col_scale[None, None, :]


def draw_gradient(key, part):
    key = jax.random.fold_in(key, 23)
    key_noise, key_rows, key_cols = jax.random.split(key, 3)
    noise = jnp.clip(jax.random.normal(key_noise, (REPLICAS, ROWS, COLS), jnp.float32), -4.0, 4.0)
    row_scale = scales(key_rows, ROWS, 1.1513)
    col_scale = scales(key_cols, COLS, 1.1513)
    return (noise * row_scale[None, :, None] * col_scale[None, None, :]).astype(jnp.bfloat16)


def draw_right_in(key, part):
    basis = column_basis(key)
    key = jax.random.fold_in(key, 37)
    extra = 0.5 * jnp.clip(jax.random.normal(key, (COLS, RANK), jnp.float32), -4.0, 4.0)
    return basis + extra


def setup_inputs(seed: int = 0) -> dict:
    key_of = jax.random.split(jax.random.key(seed), 4)
    return {
        "momentum": draw_momentum(jax.random.fold_in(key_of[3], 71), 0),
        "gradient": draw_gradient(jax.random.fold_in(key_of[3], 71), 0),
        "right_in": draw_right_in(jax.random.fold_in(key_of[3], 71), 0),
    }


def reference(momentum, gradient, right_in):
    highest = lax.Precision.HIGHEST
    projected = jnp.zeros((ROWS, RANK), jnp.float32)
    for replica_index in range(REPLICAS):
        buffer = momentum[replica_index] + gradient[replica_index].astype(jnp.float32)
        projected = projected + jnp.dot(buffer, right_in, precision=highest)
    projected = projected / REPLICAS
    gram_matrix = jnp.dot(projected.T, projected, precision=highest)
    factor_low = jnp.linalg.cholesky(gram_matrix)
    orthonormal = jax.scipy.linalg.solve_triangular(factor_low, projected.T, lower=True).T
    back_proj = jnp.zeros((COLS, RANK), jnp.float32)
    for replica_index in range(REPLICAS):
        buffer = momentum[replica_index] + gradient[replica_index].astype(jnp.float32)
        back_proj = back_proj + jnp.dot(buffer.T, orthonormal, precision=highest)
    back_proj = back_proj / REPLICAS
    column_norm = jnp.sqrt(lax.optimization_barrier(jnp.sum(back_proj * back_proj, axis=0)) + 1e-06)
    right_factor = back_proj * (math.sqrt(COLS) / column_norm)[None, :]
    left_factor = orthonormal * math.sqrt(ROWS)
    correction = 0.1 * jnp.dot(orthonormal, back_proj.T, precision=highest)
    updated = []
    for replica_index in range(REPLICAS):
        buffer = momentum[replica_index] + gradient[replica_index].astype(jnp.float32)
        updated.append(buffer - correction)
    return (left_factor, right_factor, jnp.stack(updated))
```

```python
import math

import jax
import jax.numpy as jnp
from jax import lax
from jax.sharding import PartitionSpec as P

HIGHEST = lax.Precision.HIGHEST
GROUP = ("replica", "tensor")


def spread(block, axes, count):
    copies = jnp.broadcast_to(block[None], (count,) + block.shape)
    return lax.all_to_all(copies, axes, 0, 0, tiled=True)


def inverse_factor(gram_matrix):
    factor_low = jnp.linalg.cholesky(gram_matrix)
    unit = jnp.eye(gram_matrix.shape[0], dtype=jnp.float32)
    return jax.scipy.linalg.solve_triangular(factor_low, unit, lower=True)


def shards(momentum, gradient, right_in):
    buffer = momentum[0] + gradient[0].astype(jnp.float32)
    row_count, col_count = buffer.shape
    rank = right_in.shape[1]
    replicas = lax.axis_size("replica")
    fsdp_count = lax.axis_size("fsdp")
    tensor_count = lax.axis_size("tensor")
    group_count = replicas * tensor_count
    replica = lax.axis_index("replica")
    place = replica * tensor_count + lax.axis_index("tensor")
    own = right_in.shape[0]
    piece = own // replicas
    quarter = piece * fsdp_count
    slab = rank // group_count
    band = row_count // group_count

    right_piece = lax.dynamic_slice_in_dim(right_in, replica * piece, piece, 0)
    right_quarter = spread(right_piece, "fsdp", fsdp_count).reshape(quarter, rank)
    turned = buffer.T.reshape(fsdp_count, replicas, piece, row_count)
    turned = turned.transpose(1, 0, 2, 3).reshape(col_count, row_count)
    mean_quarter = lax.psum_scatter(turned, "replica", scatter_dimension=0, tiled=True) / replicas

    partial_value = lax.dot_general(
        mean_quarter, right_quarter, (((0,), (0,)), ((), ())), precision=HIGHEST
    )
    partial_value = partial_value.reshape(group_count, band, rank)
    partial_value = lax.all_to_all(partial_value, GROUP, 0, 0, tiled=True)
    projected = spread(jnp.sum(partial_value, axis=0), GROUP, group_count).reshape(row_count, rank)

    gram_terms = lax.dot_general(projected, projected, (((0,), (0,)), ((), ())), precision=HIGHEST)
    gram_slab = lax.dynamic_slice_in_dim(gram_terms, place * slab, slab, 0)
    raw_terms = jnp.dot(mean_quarter, projected, precision=HIGHEST)
    terms = jnp.concatenate(
        [
            raw_terms.reshape(fsdp_count, piece, rank),
            jnp.broadcast_to(gram_slab[None], (fsdp_count, slab, rank)),
        ],
        axis=1,
    )
    sums = jnp.sum(lax.all_to_all(terms, "fsdp", 0, 0, tiled=True), axis=0)
    raw_own, gram_slab = sums[:piece], sums[piece:]
    raw_quarter = spread(raw_own, "fsdp", fsdp_count).reshape(quarter, rank)
    gram_matrix = spread(gram_slab, GROUP, group_count).reshape(rank, rank)

    inverse = inverse_factor(gram_matrix)
    orthonormal = jnp.dot(projected, inverse.T, precision=HIGHEST)
    back_quarter = jnp.dot(raw_quarter, inverse.T, precision=HIGHEST)
    back = lax.all_gather(back_quarter, "replica", axis=0, tiled=False)
    squares = jnp.sum(back_quarter * back_quarter, axis=0)[None]
    squares = jnp.sum(spread(squares, GROUP, group_count), axis=(0, 1))
    back = back.reshape(replicas, fsdp_count, piece, rank).transpose(1, 0, 2, 3)
    column_norm = jnp.sqrt(squares + 1e-06)
    own_rows = lax.dynamic_index_in_dim(back, lax.axis_index("fsdp"), 0, False).reshape(own, rank)
    right_factor = own_rows * (math.sqrt(col_count * tensor_count) / column_norm)[None, :]
    left_factor = orthonormal * math.sqrt(row_count * fsdp_count)
    back = back.reshape(col_count, rank)
    new_momentum = buffer - 0.1 * jnp.dot(orthonormal, back.T, precision=HIGHEST)
    return (left_factor, right_factor, new_momentum[None])


def solution(mesh):
    placed = (
        P("replica", "fsdp", "tensor"),
        P("replica", "fsdp", "tensor"),
        P(("tensor", "fsdp"), None),
    )
    return jax.shard_map(
        shards,
        mesh=mesh,
        in_specs=placed,
        out_specs=(P("fsdp", None), P(("tensor", "fsdp"), None), P("replica", "fsdp", "tensor")),
        check_vma=False,
    )
```

```python
import functools
import math

import jax
import jax.numpy as jnp
from jax import lax
from jax.experimental import pallas as pl
from jax.experimental.pallas import tpu as pltpu
from jax.sharding import PartitionSpec as P

HIGHEST = lax.Precision.HIGHEST
GROUP = ("replica", "tensor")
PANEL = 64
NEAR = 4
LANES = 128
VMEM_LIMIT = 40 * 1024 * 1024
VMEM_WHOLE = 63 * 1024 * 1024


def exchange(blocks, axes, groups=None):
    return lax.all_to_all(blocks, axes, 0, 0, tiled=True, axis_index_groups=groups)


def pack(value):
    return jnp.concatenate([value[:, :LANES], value[:, LANES:]], axis=0)


def unpack(value):
    half = value.shape[0] // 2
    return jnp.concatenate([value[:half], value[half:]], axis=1)


def column_dot(left, right):
    return lax.dot_general(
        left, right, (((0,), (0,)), ((), ())), precision=HIGHEST, preferred_element_type=jnp.float32
    )


def row_dot(left, right):
    return lax.dot_general(
        left, right, (((1,), (1,)), ((), ())), precision=HIGHEST, preferred_element_type=jnp.float32
    )


def turn_kernel(where_ref, momentum_ref, gradient_ref, right_ref, *refs):
    outs, copies_ref, sorted_rows = refs[:-2], refs[-2], refs[-1]
    replica = where_ref[0]
    turned = (momentum_ref[0] + gradient_ref[0].astype(jnp.float32)).T
    replicas, blocks, packed = sorted_rows.shape[:3]
    piece = packed // 2
    for block in range(blocks):
        for part in range(replicas):
            start = (block * replicas + part) * piece
            rows = turned[start : start + piece, :]
            sorted_rows[part, block, :piece, :] = rows[:, :LANES]
            sorted_rows[part, block, piece:, :] = rows[:, LANES:]
    for step, out_ref in enumerate(outs):
        out_ref[...] = sorted_rows[lax.rem(replica + step, replicas)]

    @pl.when(pl.program_id(0) == 0)
    def _():
        rows = right_ref[:piece, :]
        for part in range(1, replicas):
            rows = jnp.where(replica == part, right_ref[part * piece : (part + 1) * piece, :], rows)
        copies_ref[...] = jnp.broadcast_to(pack(rows)[None], copies_ref.shape)


def turn(where, momentum, gradient, right_in, replicas, fsdp_count):
    row_count, col_count = momentum.shape[1:]
    own = col_count // fsdp_count
    group = math.lcm(own, LANES)
    steps = col_count // group
    packed = 2 * (own // replicas)
    block = (fsdp_count // steps, packed, LANES)
    whole = (fsdp_count, packed, LANES)
    return pl.pallas_call(
        turn_kernel,
        grid=(steps,),
        in_specs=[pl.BlockSpec(memory_space=pltpu.SMEM)]
        + [pl.BlockSpec((1, row_count, group), lambda i: (0, 0, i))] * 2
        + [pl.BlockSpec(right_in.shape, lambda i: (0, 0))],
        out_specs=[pl.BlockSpec(block, lambda i: (i, 0, 0))] * replicas
        + [pl.BlockSpec(whole, lambda i: (0, 0, 0))],
        out_shape=[jax.ShapeDtypeStruct(whole, jnp.float32)] * (replicas + 1),
        scratch_shapes=[pltpu.VMEM((replicas,) + block, jnp.float32)],
        compiler_params=pltpu.CompilerParams(vmem_limit_bytes=VMEM_WHOLE),
        name="turn",
    )(where, momentum, gradient, right_in)


def project_kernel(part_refs, right_ref, sum_ref, out_ref, right):
    blocks, packed = right_ref.shape[:2]
    piece = packed // 2
    for block in range(blocks):
        total = part_refs[0][block]
        for part_ref in part_refs[1:]:
            total = total + part_ref[block]
        rows = slice(block * piece, (block + 1) * piece)
        sum_ref[rows, :] = unpack(total)
        right[rows, :] = unpack(right_ref[block])
    out_ref[...] = column_dot(sum_ref[...], right[...])


def project(parts, right_quarter):
    def body(*refs):
        project_kernel(refs[: len(parts)], *refs[len(parts) :])

    blocks, packed, _ = right_quarter.shape
    quarter, rank = blocks * packed // 2, 2 * LANES
    return pl.pallas_call(
        body,
        out_shape=[
            jax.ShapeDtypeStruct((quarter, 2 * LANES), jnp.float32),
            jax.ShapeDtypeStruct((2 * LANES, rank), jnp.float32),
        ],
        scratch_shapes=[pltpu.VMEM((quarter, rank), jnp.float32)],
        compiler_params=pltpu.CompilerParams(vmem_limit_bytes=VMEM_LIMIT),
        name="project",
    )(*parts, right_quarter)


def sum_copies_kernel(scale, blocks_ref, out_ref):
    total = jnp.sum(blocks_ref[...], axis=0, keepdims=True) * scale
    out_ref[...] = jnp.broadcast_to(total, out_ref.shape)


def sum_copies(blocks, scale):
    return pl.pallas_call(
        functools.partial(sum_copies_kernel, scale),
        out_shape=jax.ShapeDtypeStruct(blocks.shape, jnp.float32),
        compiler_params=pltpu.CompilerParams(vmem_limit_bytes=VMEM_LIMIT),
        name="sum_copies",
    )(blocks)


def sum_kernel(blocks_ref, out_ref):
    rows = out_ref.shape[1]
    for receiver in range(out_ref.shape[0]):
        part = slice(receiver * rows, (receiver + 1) * rows)
        total = blocks_ref[0, part, :]
        for sender in range(1, blocks_ref.shape[0]):
            total = total + blocks_ref[sender, part, :]
        out_ref[receiver] = total


def sum_blocks(blocks, receivers):
    rows = blocks.shape[1] // receivers
    return pl.pallas_call(
        sum_kernel,
        out_shape=jax.ShapeDtypeStruct((receivers, rows, LANES), jnp.float32),
        compiler_params=pltpu.CompilerParams(vmem_limit_bytes=VMEM_LIMIT),
        name="sum_blocks",
    )(blocks)


def terms_kernel(share, where_ref, sum_ref, projected_ref, out_ref, gram):
    near, far, packed = out_ref.shape[:3]
    blocks = near * far
    piece = sum_ref.shape[0] // blocks
    slab = share * blocks
    projected = projected_ref[...]
    gram[...] = column_dot(projected, projected)
    rows = gram[pl.ds(pl.multiple_of(where_ref[2] * slab, slab), slab), :]
    raw = jnp.dot(
        sum_ref[...], projected, precision=HIGHEST, preferred_element_type=jnp.float32
    )
    rest = jnp.zeros((packed - 2 * (piece + share), LANES), jnp.float32)
    for block in range(blocks):
        a, b = divmod(block, near)
        out_ref[b, a, : 2 * piece, :] = pack(raw[block * piece : (block + 1) * piece, :])
        tail = pack(rows[block * share : (block + 1) * share, :])
        out_ref[b, a, 2 * piece :, :] = jnp.concatenate([tail, rest], axis=0)


def make_terms(where, column_sum, projected, blocks, tensor_count):
    rank = projected.shape[1]
    share = rank // tensor_count // blocks
    packed = 2 * (column_sum.shape[0] // blocks + share)
    whole = pl.BlockSpec(memory_space=pltpu.VMEM)
    return pl.pallas_call(
        functools.partial(terms_kernel, share),
        in_specs=[pl.BlockSpec(memory_space=pltpu.SMEM), whole, whole],
        out_specs=whole,
        out_shape=jax.ShapeDtypeStruct((NEAR, blocks // NEAR, -(-packed // 8) * 8, LANES), jnp.float32),
        scratch_shapes=[pltpu.VMEM((rank, rank), jnp.float32)],
        compiler_params=pltpu.CompilerParams(vmem_limit_bytes=VMEM_LIMIT),
        name="terms",
    )(where, column_sum, projected)


def slab_kernel(packed, sums_ref, slab_ref):
    near, far = sums_ref.shape[:2]
    share = slab_ref.shape[1] // (near * far)
    tail = slice(packed, packed + 2 * share)
    rows = [unpack(sums_ref[b, a, tail, :]) for a in range(far) for b in range(near)]
    slab_ref[...] = jnp.broadcast_to(jnp.concatenate(rows, axis=0)[None], slab_ref.shape)


def take_slab(sums, packed, slab, tensor_count):
    return pl.pallas_call(
        functools.partial(slab_kernel, packed),
        out_shape=jax.ShapeDtypeStruct((tensor_count, slab, 2 * LANES), jnp.float32),
        compiler_params=pltpu.CompilerParams(vmem_limit_bytes=VMEM_LIMIT),
        name="slab",
    )(sums)


def raw_kernel(sums_ref, raw_ref):
    near = sums_ref.shape[0]
    for block in range(raw_ref.shape[0]):
        a, b = divmod(block, near)
        raw_ref[block] = sums_ref[b, a, : raw_ref.shape[1], :]


def take_raw(sums, packed):
    near, far = sums.shape[:2]
    return pl.pallas_call(
        raw_kernel,
        out_shape=jax.ShapeDtypeStruct((near * far, packed, LANES), jnp.float32),
        compiler_params=pltpu.CompilerParams(vmem_limit_bytes=VMEM_LIMIT),
        name="raw",
    )(sums)


def invert_factor(work, inverse_ref):
    rank = work.shape[0]
    lane = lax.broadcasted_iota(jnp.int32, (PANEL, rank), 1)
    row = lax.broadcasted_iota(jnp.int32, (PANEL, rank), 0)
    lane8, row8 = lane[:8, :LANES], row[:8, :LANES]
    tiles = rank // LANES
    groups = PANEL // 8

    def every(value):
        return jnp.broadcast_to(value, (8, LANES))

    for panel in range(0, rank, PANEL):
        rows = [
            [
                work[panel + 8 * h : panel + 8 * h + 8, LANES * t : LANES * (t + 1)]
                for t in range(tiles)
            ]
            for h in range(groups)
        ]
        inverses = []
        for g in range(groups):
            tile, start = divmod(panel + 8 * g, LANES)
            shares = {
                h: [every(rows[h][tile][:, start + j : start + j + 1]) for j in range(8)]
                for h in range(g, groups)
            }
            pivot_rows = [[every(rows[g][t][j : j + 1]) for j in range(8)] for t in range(tiles)]
            pivot_inverses = None
            for k in range(8):
                inverse = 1.0 / every(shares[g][k][k : k + 1])
                if pivot_inverses is None:
                    pivot_inverses = inverse
                else:
                    pivot_inverses = jnp.where(row8 == k, inverse, pivot_inverses)
                pivot_row = [every(shares[g][j][k : k + 1]) for j in range(8)]
                for h in range(g, groups):
                    factor = shares[h][k] * inverse
                    if h == g:
                        factor = jnp.where(row8 > k, factor, 0.0)
                    for j in range(8):
                        if j != k:
                            shares[h][j] = shares[h][j] - factor * pivot_row[j]
                    shares[h][k] = jnp.where(row8 == k, 1.0, -factor) if h == g else -factor
            inverses.append(pivot_inverses)
            shares[g] = [jnp.where(row8 >= j, shares[g][j], 0.0) for j in range(8)]
            for h in range(groups - 1, g - 1, -1):
                for t in range(tiles):
                    products = [shares[h][j] * pivot_rows[t][j] for j in range(8)]
                    while len(products) > 1:
                        products = [a + b for a, b in zip(products[::2], products[1::2])]
                    total = products[0] if h == g else rows[h][t] + products[0]
                    if t == tile:
                        for j in range(8):
                            total = jnp.where(lane8 == start + j, shares[h][j], total)
                    rows[h][t] = total
        whole = jnp.concatenate([jnp.concatenate(r, axis=1) for r in rows], axis=0)
        scale = jnp.concatenate([jnp.concatenate([r] * tiles, axis=1) for r in inverses], axis=0)
        unit = jnp.where((lane > panel + row) & (lane < panel + PANEL), 0.0, whole)
        inverse_ref[panel : panel + PANEL, :] = jnp.where(lane <= panel + row, unit, 0.0) * jnp.sqrt(scale)
        below = panel + PANEL
        if below < rank:
            rest = work[below:, :]
            lanes = lax.broadcasted_iota(jnp.int32, rest.shape, 1)
            rest = jnp.where((lanes >= panel) & (lanes < below), 0.0, rest)
            first = below // LANES * LANES
            work[below:, :] = rest - column_dot((whole * scale)[:, first:], unit)[below - first :]


def factor_kernel(
    replicas, rows, gram_ref, projected_ref, raw_ref, inverse_ref, ortho_ref, left_ref, squares_ref, work, raw
):
    blocks, packed = raw_ref.shape[:2]
    piece = packed // 2
    for block in range(blocks):
        raw[block * piece : (block + 1) * piece, :] = unpack(raw_ref[block])
    work[...] = gram_ref[...]
    invert_factor(work, inverse_ref)
    inverse = inverse_ref[...]
    ortho = row_dot(projected_ref[...], inverse)
    ortho_ref[...] = jnp.dot(
        ortho, inverse, precision=HIGHEST, preferred_element_type=jnp.float32
    ) * (1.0 / replicas)
    left_ref[...] = ortho * math.sqrt(rows)
    inverse = inverse * (1.0 / replicas)
    inverse_ref[...] = inverse
    back = row_dot(raw[...], inverse)
    squares = pack(jnp.sum(back * back, axis=0, keepdims=True))
    rest = jnp.zeros((squares_ref.shape[1] - 2, LANES), jnp.float32)
    squares_ref[...] = jnp.broadcast_to(jnp.concatenate([squares, rest], axis=0)[None], squares_ref.shape)


def make_factor(gram_matrix, projected, raw_quarter, replicas, rows, group_count):
    rank = gram_matrix.shape[0]
    blocks, packed, _ = raw_quarter.shape
    return pl.pallas_call(
        functools.partial(factor_kernel, replicas, rows),
        out_shape=[
            jax.ShapeDtypeStruct(gram_matrix.shape, jnp.float32),
            jax.ShapeDtypeStruct(projected.shape, jnp.float32),
            jax.ShapeDtypeStruct(projected.shape, jnp.float32),
            jax.ShapeDtypeStruct((group_count, 8, LANES), jnp.float32),
        ],
        scratch_shapes=[
            pltpu.VMEM(gram_matrix.shape, jnp.float32),
            pltpu.VMEM((blocks * packed // 2, rank), jnp.float32),
        ],
        compiler_params=pltpu.CompilerParams(vmem_limit_bytes=VMEM_LIMIT),
        cost_estimate=pl.CostEstimate(flops=3 * 10**10, bytes_accessed=10**6, transcendentals=0),
        name="factor",
    )(gram_matrix, projected, raw_quarter)


def update_kernel(where_ref, momentum_ref, gradient_ref, ortho_ref, inverse_ref, *refs):
    parts, (out_ref, own_ref, sorted_rows, raw) = refs[:-4], refs[-4:]
    replicas, blocks, packed = sorted_rows.shape[:3]
    piece = packed // 2
    own = replicas * piece
    for step, part_ref in enumerate(parts):
        sorted_rows[lax.rem(where_ref[0] + step, replicas)] = part_ref[...]
    for block in range(blocks):
        for replica in range(replicas):
            start = block * own + replica * piece
            raw[start : start + piece, :] = unpack(sorted_rows[replica, block])
    correction = row_dot(ortho_ref[...], raw[...])
    out_ref[0] = momentum_ref[0] + gradient_ref[0].astype(jnp.float32) - 0.1 * correction

    @pl.when(where_ref[1] // blocks == pl.program_id(0))
    def _():
        start = pl.multiple_of(lax.rem(where_ref[1], blocks) * own, 8)
        own_ref[...] = row_dot(raw[pl.ds(start, own), :], inverse_ref[...])


def update(where, momentum, gradient, orthonormal, inverse, parts):
    row_count, own_count = momentum.shape[1:]
    replicas = len(parts)
    fsdp_count, packed, _ = parts[0].shape
    rank = orthonormal.shape[1]
    own = own_count // fsdp_count
    group = math.lcm(own, LANES)
    steps = own_count // group
    columns = pl.BlockSpec((1, row_count, group), lambda i: (0, 0, i))
    block = (fsdp_count // steps, packed, LANES)
    return pl.pallas_call(
        update_kernel,
        grid=(steps,),
        in_specs=[
            pl.BlockSpec(memory_space=pltpu.SMEM),
            columns,
            columns,
            pl.BlockSpec((row_count, rank), lambda i: (0, 0)),
            pl.BlockSpec((rank, rank), lambda i: (0, 0)),
        ]
        + [pl.BlockSpec(block, lambda i: (i, 0, 0))] * replicas,
        out_specs=[columns, pl.BlockSpec((own, rank), lambda i: (0, 0))],
        out_shape=[
            jax.ShapeDtypeStruct(momentum.shape, jnp.float32),
            jax.ShapeDtypeStruct((own, rank), jnp.float32),
        ],
        scratch_shapes=[
            pltpu.VMEM((replicas,) + block, jnp.float32),
            pltpu.VMEM((group, rank), jnp.float32),
        ],
        compiler_params=pltpu.CompilerParams(vmem_limit_bytes=VMEM_WHOLE),
        name="update",
    )(where, momentum, gradient, orthonormal, inverse, *parts)


def scale_kernel(columns, own_ref, squares_ref, out_ref):
    squares = unpack(jnp.sum(squares_ref[...], axis=0)[:2])
    out_ref[...] = own_ref[...] * (math.sqrt(columns) / jnp.sqrt(squares + 1e-06))


def make_right(own_rows, squares, columns):
    return pl.pallas_call(
        functools.partial(scale_kernel, columns),
        out_shape=jax.ShapeDtypeStruct(own_rows.shape, jnp.float32),
        compiler_params=pltpu.CompilerParams(vmem_limit_bytes=VMEM_LIMIT),
        name="scale",
    )(own_rows, squares)


def shards(momentum, gradient, right_in):
    row_count, col_count = momentum.shape[1:]
    rank = right_in.shape[1]
    replicas = lax.axis_size("replica")
    fsdp_count = lax.axis_size("fsdp")
    tensor_count = lax.axis_size("tensor")
    group_count = replicas * tensor_count
    where = jnp.stack([lax.axis_index("replica"), lax.axis_index("fsdp"), lax.axis_index("tensor")])
    band = row_count // group_count
    packed = 2 * (col_count // fsdp_count // replicas)
    slab = rank // tensor_count
    far = fsdp_count // NEAR
    near_groups = [[a * NEAR + b for b in range(NEAR)] for a in range(far)]
    far_groups = [[a * NEAR + b for a in range(far)] for b in range(NEAR)]

    def around(value, step):
        pairs = [(i, (i + step) % replicas) for i in range(replicas)]
        return lax.ppermute(value, "replica", pairs)

    *turned, right_copies = turn(where, momentum, gradient, right_in, replicas, fsdp_count)
    right_quarter = exchange(right_copies, "fsdp")
    parts = [turned[0]] + [around(turned[step], step) for step in range(1, replicas)]
    column_sum, partial_value = project(parts, right_quarter)

    partial_value = exchange(partial_value.reshape(group_count, band, rank), GROUP)
    projected = exchange(sum_copies(partial_value, 1.0 / replicas), GROUP).reshape(row_count, rank)

    terms = make_terms(where, column_sum, projected, fsdp_count, tensor_count)
    height = terms.shape[2]
    terms = exchange(terms.reshape(NEAR, far * height, LANES), "fsdp", near_groups)
    sums = exchange(sum_blocks(terms, far), "fsdp", far_groups)
    sums = exchange(sum_copies(sums, 1.0), "fsdp", far_groups).reshape(1, far * height, LANES)
    sums = exchange(jnp.broadcast_to(sums, (NEAR, far * height, LANES)), "fsdp", near_groups)
    sums = sums.reshape(NEAR, far, height, LANES)
    gram_matrix = exchange(take_slab(sums, packed, slab, tensor_count), "tensor").reshape(rank, rank)
    raw_quarter = take_raw(sums, packed)
    raw_parts = [raw_quarter] + [around(raw_quarter, -step) for step in range(1, replicas)]
    inverse, combined, left_factor, squares = make_factor(
        gram_matrix, projected, raw_quarter, replicas, row_count * fsdp_count, group_count
    )
    new_momentum, own_rows = update(where, momentum, gradient, combined, inverse, raw_parts)
    right_factor = make_right(own_rows, exchange(squares, GROUP), col_count * tensor_count)
    return (left_factor, right_factor, new_momentum)


def solution(mesh):
    placed = (
        P("replica", "fsdp", "tensor"),
        P("replica", "fsdp", "tensor"),
        P(("tensor", "fsdp"), None),
    )
    return jax.shard_map(
        shards,
        mesh=mesh,
        in_specs=placed,
        out_specs=(P("fsdp", None), P(("tensor", "fsdp"), None), P("replica", "fsdp", "tensor")),
        check_vma=False,
    )
```

```python
import functools
import math

import jax
import jax.numpy as jnp
from jax import lax
from jax.experimental import pallas as pl
from jax.experimental.pallas import tpu as pltpu
from jax.sharding import PartitionSpec as P

HIGHEST = lax.Precision.HIGHEST
GROUP = ("replica", "tensor")
PANEL = 64
NEAR = 4
LANES = 128
VMEM_LIMIT = 20 * 1024 * 1024
VMEM_WHOLE = 63 * 1024 * 1024


def exchange(blocks, axes, groups=None):
    return lax.all_to_all(blocks, axes, 0, 0, tiled=True, axis_index_groups=groups)


def pack(value):
    return jnp.concatenate([value[:, :LANES], value[:, LANES:]], axis=0)


def unpack(value):
    half = value.shape[0] // 2
    return jnp.concatenate([value[:half], value[half:]], axis=1)


def column_dot(left, right):
    return lax.dot_general(
        left, right, (((0,), (0,)), ((), ())), precision=HIGHEST, preferred_element_type=jnp.float32
    )


def row_dot(left, right):
    return lax.dot_general(
        left, right, (((1,), (1,)), ((), ())), precision=HIGHEST, preferred_element_type=jnp.float32
    )


def turn_kernel(momentum_ref, gradient_ref, right_ref, *refs):
    outs, (copies_ref, buffer_ref, sorted_rows) = refs[:-3], refs[-3:]
    replica = lax.axis_index("replica")
    buffer = momentum_ref[0] + gradient_ref[0].astype(jnp.float32)
    buffer_ref[0] = buffer
    turned = buffer.T
    replicas, blocks, packed = sorted_rows.shape[:3]
    piece = packed // 2
    for block in range(blocks):
        for part in range(replicas):
            start = (block * replicas + part) * piece
            rows = turned[start : start + piece, :]
            sorted_rows[part, block, :piece, :] = rows[:, :LANES]
            sorted_rows[part, block, piece:, :] = rows[:, LANES:]
    for step, out_ref in enumerate(outs):
        out_ref[...] = sorted_rows[lax.rem(replica + step, replicas)]

    @pl.when(pl.program_id(0) == 0)
    def _():
        rows = right_ref[:piece, :]
        for part in range(1, replicas):
            rows = jnp.where(replica == part, right_ref[part * piece : (part + 1) * piece, :], rows)
        copies_ref[...] = jnp.broadcast_to(pack(rows)[None], copies_ref.shape)


def turn(momentum, gradient, right_in, replicas, fsdp_count):
    row_count, col_count = momentum.shape[1:]
    own = col_count // fsdp_count
    group = math.lcm(own, LANES)
    steps = col_count // group
    packed = 2 * (own // replicas)
    block = (fsdp_count // steps, packed, LANES)
    whole = (fsdp_count, packed, LANES)
    columns = pl.BlockSpec((1, row_count, group), lambda i: (0, 0, i))
    return pl.pallas_call(
        turn_kernel,
        grid=(steps,),
        in_specs=[columns] * 2 + [pl.BlockSpec(right_in.shape, lambda i: (0, 0))],
        out_specs=[pl.BlockSpec(block, lambda i: (i, 0, 0))] * replicas
        + [pl.BlockSpec(whole, lambda i: (0, 0, 0)), columns],
        out_shape=[jax.ShapeDtypeStruct(whole, jnp.float32)] * (replicas + 1)
        + [jax.ShapeDtypeStruct(momentum.shape, jnp.float32)],
        scratch_shapes=[pltpu.VMEM((replicas,) + block, jnp.float32)],
        compiler_params=pltpu.CompilerParams(vmem_limit_bytes=VMEM_WHOLE),
        name="turn",
    )(momentum, gradient, right_in)


def project_kernel(part_refs, right_ref, sum_ref, out_ref, right):
    blocks, packed = right_ref.shape[:2]
    piece = packed // 2
    for block in range(blocks):
        total = part_refs[0][block]
        for part_ref in part_refs[1:]:
            total = total + part_ref[block]
        rows = slice(block * piece, (block + 1) * piece)
        sum_ref[rows, :] = unpack(total)
        right[rows, :] = unpack(right_ref[block])
    out_ref[...] = column_dot(sum_ref[...], right[...])


def project(parts, right_quarter):
    def body(*refs):
        project_kernel(refs[: len(parts)], *refs[len(parts) :])

    blocks, packed, _ = right_quarter.shape
    quarter, rank = blocks * packed // 2, 2 * LANES
    return pl.pallas_call(
        body,
        out_shape=[
            jax.ShapeDtypeStruct((quarter, 2 * LANES), jnp.float32),
            jax.ShapeDtypeStruct((2 * LANES, rank), jnp.float32),
        ],
        scratch_shapes=[pltpu.VMEM((quarter, rank), jnp.float32)],
        compiler_params=pltpu.CompilerParams(vmem_limit_bytes=VMEM_LIMIT),
        name="project",
    )(*parts, right_quarter)


def sum_copies_kernel(scale, blocks_ref, out_ref):
    total = jnp.sum(blocks_ref[...], axis=0, keepdims=True) * scale
    out_ref[...] = jnp.broadcast_to(total, out_ref.shape)


def sum_copies(blocks, scale):
    return pl.pallas_call(
        functools.partial(sum_copies_kernel, scale),
        out_shape=jax.ShapeDtypeStruct(blocks.shape, jnp.float32),
        compiler_params=pltpu.CompilerParams(vmem_limit_bytes=VMEM_LIMIT),
        name="sum_copies",
    )(blocks)


def sum_kernel(blocks_ref, out_ref):
    rows = out_ref.shape[1]
    for receiver in range(out_ref.shape[0]):
        part = slice(receiver * rows, (receiver + 1) * rows)
        total = blocks_ref[0, part, :]
        for sender in range(1, blocks_ref.shape[0]):
            total = total + blocks_ref[sender, part, :]
        out_ref[receiver] = total


def sum_blocks(blocks, receivers):
    rows = blocks.shape[1] // receivers
    return pl.pallas_call(
        sum_kernel,
        out_shape=jax.ShapeDtypeStruct((receivers, rows, LANES), jnp.float32),
        compiler_params=pltpu.CompilerParams(vmem_limit_bytes=VMEM_LIMIT),
        name="sum_blocks",
    )(blocks)


def terms_kernel(share, sum_ref, projected_ref, out_ref, gram):
    near, far, packed = out_ref.shape[:3]
    blocks = near * far
    piece = sum_ref.shape[0] // blocks
    slab = share * blocks
    projected = projected_ref[...]
    gram[...] = column_dot(projected, projected)
    rows = gram[pl.ds(pl.multiple_of(lax.axis_index("tensor") * slab, slab), slab), :]
    raw = jnp.dot(
        sum_ref[...], projected, precision=HIGHEST, preferred_element_type=jnp.float32
    )
    rest = jnp.zeros((packed - 2 * (piece + share), LANES), jnp.float32)
    for block in range(blocks):
        a, b = divmod(block, near)
        out_ref[b, a, : 2 * piece, :] = pack(raw[block * piece : (block + 1) * piece, :])
        tail = pack(rows[block * share : (block + 1) * share, :])
        out_ref[b, a, 2 * piece :, :] = jnp.concatenate([tail, rest], axis=0)


def make_terms(column_sum, projected, blocks, tensor_count):
    rank = projected.shape[1]
    share = rank // tensor_count // blocks
    packed = 2 * (column_sum.shape[0] // blocks + share)
    return pl.pallas_call(
        functools.partial(terms_kernel, share),
        out_shape=jax.ShapeDtypeStruct((NEAR, blocks // NEAR, -(-packed // 8) * 8, LANES), jnp.float32),
        scratch_shapes=[pltpu.VMEM((rank, rank), jnp.float32)],
        compiler_params=pltpu.CompilerParams(vmem_limit_bytes=VMEM_LIMIT),
        name="terms",
    )(column_sum, projected)


def slab_kernel(packed, sums_ref, slab_ref):
    near, far = sums_ref.shape[:2]
    share = slab_ref.shape[1] // (near * far)
    tail = slice(packed, packed + 2 * share)
    rows = [unpack(sums_ref[b, a, tail, :]) for a in range(far) for b in range(near)]
    slab_ref[...] = jnp.broadcast_to(jnp.concatenate(rows, axis=0)[None], slab_ref.shape)


def take_slab(sums, packed, slab, tensor_count):
    return pl.pallas_call(
        functools.partial(slab_kernel, packed),
        out_shape=jax.ShapeDtypeStruct((tensor_count, slab, 2 * LANES), jnp.float32),
        compiler_params=pltpu.CompilerParams(vmem_limit_bytes=VMEM_LIMIT),
        name="slab",
    )(sums)


def raw_kernel(sums_ref, raw_ref):
    near = sums_ref.shape[0]
    for block in range(raw_ref.shape[0]):
        a, b = divmod(block, near)
        raw_ref[block] = sums_ref[b, a, : raw_ref.shape[1], :]


def take_raw(sums, packed):
    near, far = sums.shape[:2]
    return pl.pallas_call(
        raw_kernel,
        out_shape=jax.ShapeDtypeStruct((near * far, packed, LANES), jnp.float32),
        compiler_params=pltpu.CompilerParams(vmem_limit_bytes=VMEM_LIMIT),
        name="raw",
    )(sums)


def invert_factor(work, inverse_ref):
    rank = work.shape[0]
    lane = lax.broadcasted_iota(jnp.int32, (PANEL, rank), 1)
    row = lax.broadcasted_iota(jnp.int32, (PANEL, rank), 0)
    lane8, row8 = lane[:8, :LANES], row[:8, :LANES]
    tiles = rank // LANES
    groups = PANEL // 8

    def every(value):
        return jnp.broadcast_to(value, (8, LANES))

    for panel in range(0, rank, PANEL):
        rows = [
            [
                work[panel + 8 * h : panel + 8 * h + 8, LANES * t : LANES * (t + 1)]
                for t in range(tiles)
            ]
            for h in range(groups)
        ]
        inverses = []
        for g in range(groups):
            tile, start = divmod(panel + 8 * g, LANES)
            shares = {
                h: [every(rows[h][tile][:, start + j : start + j + 1]) for j in range(8)]
                for h in range(g, groups)
            }
            pivot_rows = [[every(rows[g][t][j : j + 1]) for j in range(8)] for t in range(tiles)]
            pivot_inverses = None
            for k in range(8):
                inverse = 1.0 / every(shares[g][k][k : k + 1])
                if pivot_inverses is None:
                    pivot_inverses = inverse
                else:
                    pivot_inverses = jnp.where(row8 == k, inverse, pivot_inverses)
                pivot_row = [every(shares[g][j][k : k + 1]) for j in range(8)]
                for h in range(g, groups):
                    factor = shares[h][k] * inverse
                    if h == g:
                        factor = jnp.where(row8 > k, factor, 0.0)
                    for j in range(8):
                        if j != k:
                            shares[h][j] = shares[h][j] - factor * pivot_row[j]
                    shares[h][k] = jnp.where(row8 == k, 1.0, -factor) if h == g else -factor
            inverses.append(pivot_inverses)
            shares[g] = [jnp.where(row8 >= j, shares[g][j], 0.0) for j in range(8)]
            for h in range(groups - 1, g - 1, -1):
                for t in range(tiles):
                    products = [shares[h][j] * pivot_rows[t][j] for j in range(8)]
                    while len(products) > 1:
                        products = [a + b for a, b in zip(products[::2], products[1::2])]
                    total = products[0] if h == g else rows[h][t] + products[0]
                    if t == tile:
                        for j in range(8):
                            total = jnp.where(lane8 == start + j, shares[h][j], total)
                    rows[h][t] = total
        whole = jnp.concatenate([jnp.concatenate(r, axis=1) for r in rows], axis=0)
        scale = jnp.concatenate([jnp.concatenate([r] * tiles, axis=1) for r in inverses], axis=0)
        unit = jnp.where((lane > panel + row) & (lane < panel + PANEL), 0.0, whole)
        inverse_ref[panel : panel + PANEL, :] = jnp.where(lane <= panel + row, unit, 0.0) * jnp.sqrt(scale)
        below = panel + PANEL
        if below < rank:
            rest = work[below:, :]
            lanes = lax.broadcasted_iota(jnp.int32, rest.shape, 1)
            rest = jnp.where((lanes >= panel) & (lanes < below), 0.0, rest)
            first = below // LANES * LANES
            work[below:, :] = rest - column_dot((whole * scale)[:, first:], unit)[below - first :]


def factor_kernel(
    replicas, rows, gram_ref, projected_ref, raw_ref, inverse_ref, ortho_ref, left_ref, squares_ref, work, raw
):
    blocks, packed = raw_ref.shape[:2]
    piece = packed // 2
    for block in range(blocks):
        raw[block * piece : (block + 1) * piece, :] = unpack(raw_ref[block])
    work[...] = gram_ref[...]
    invert_factor(work, inverse_ref)
    inverse = inverse_ref[...]
    ortho = row_dot(projected_ref[...], inverse)
    ortho_ref[...] = jnp.dot(
        ortho, inverse, precision=HIGHEST, preferred_element_type=jnp.float32
    ) * (1.0 / replicas)
    left_ref[...] = ortho * math.sqrt(rows)
    inverse = inverse * (1.0 / replicas)
    inverse_ref[...] = inverse
    back = row_dot(raw[...], inverse)
    squares = pack(jnp.sum(back * back, axis=0, keepdims=True))
    rest = jnp.zeros((squares_ref.shape[1] - 2, LANES), jnp.float32)
    squares_ref[...] = jnp.broadcast_to(jnp.concatenate([squares, rest], axis=0)[None], squares_ref.shape)


def make_factor(gram_matrix, projected, raw_quarter, replicas, rows, group_count):
    rank = gram_matrix.shape[0]
    blocks, packed, _ = raw_quarter.shape
    return pl.pallas_call(
        functools.partial(factor_kernel, replicas, rows),
        out_shape=[
            jax.ShapeDtypeStruct(gram_matrix.shape, jnp.float32),
            jax.ShapeDtypeStruct(projected.shape, jnp.float32),
            jax.ShapeDtypeStruct(projected.shape, jnp.float32),
            jax.ShapeDtypeStruct((group_count, 8, LANES), jnp.float32),
        ],
        scratch_shapes=[
            pltpu.VMEM(gram_matrix.shape, jnp.float32),
            pltpu.VMEM((blocks * packed // 2, rank), jnp.float32),
        ],
        compiler_params=pltpu.CompilerParams(vmem_limit_bytes=VMEM_LIMIT),
        cost_estimate=pl.CostEstimate(flops=3 * 10**10, bytes_accessed=10**6, transcendentals=0),
        name="factor",
    )(gram_matrix, projected, raw_quarter)


def update_kernel(buffer_ref, ortho_ref, inverse_ref, *refs):
    parts, (out_ref, own_ref, sorted_rows, raw) = refs[:-4], refs[-4:]
    replicas, blocks, packed = sorted_rows.shape[:3]
    piece = packed // 2
    own = replicas * piece
    place, own_block = lax.axis_index("replica"), lax.axis_index("fsdp")
    for step, part_ref in enumerate(parts):
        sorted_rows[lax.rem(place + step, replicas)] = part_ref[...]
    for block in range(blocks):
        for replica in range(replicas):
            start = block * own + replica * piece
            raw[start : start + piece, :] = unpack(sorted_rows[replica, block])
    correction = row_dot(ortho_ref[...], raw[...])
    out_ref[0] = buffer_ref[0] - 0.1 * correction

    @pl.when(own_block // blocks == pl.program_id(0))
    def _():
        start = pl.multiple_of(lax.rem(own_block, blocks) * own, 8)
        own_ref[...] = row_dot(raw[pl.ds(start, own), :], inverse_ref[...])


def update(buffer, orthonormal, inverse, parts):
    row_count, own_count = buffer.shape[1:]
    replicas = len(parts)
    fsdp_count, packed, _ = parts[0].shape
    rank = orthonormal.shape[1]
    own = own_count // fsdp_count
    group = math.lcm(own, LANES)
    steps = own_count // group
    columns = pl.BlockSpec((1, row_count, group), lambda i: (0, 0, i))
    block = (fsdp_count // steps, packed, LANES)
    return pl.pallas_call(
        update_kernel,
        grid=(steps,),
        in_specs=[
            columns,
            pl.BlockSpec((row_count, rank), lambda i: (0, 0)),
            pl.BlockSpec((rank, rank), lambda i: (0, 0)),
        ]
        + [pl.BlockSpec(block, lambda i: (i, 0, 0))] * replicas,
        out_specs=[columns, pl.BlockSpec((own, rank), lambda i: (0, 0))],
        out_shape=[
            jax.ShapeDtypeStruct(buffer.shape, jnp.float32),
            jax.ShapeDtypeStruct((own, rank), jnp.float32),
        ],
        scratch_shapes=[
            pltpu.VMEM((replicas,) + block, jnp.float32),
            pltpu.VMEM((group, rank), jnp.float32),
        ],
        compiler_params=pltpu.CompilerParams(vmem_limit_bytes=VMEM_LIMIT),
        input_output_aliases={0: 0},
        name="update",
    )(buffer, orthonormal, inverse, *parts)


def scale_kernel(columns, own_ref, squares_ref, out_ref):
    squares = unpack(jnp.sum(squares_ref[...], axis=0)[:2])
    out_ref[...] = own_ref[...] * (math.sqrt(columns) / jnp.sqrt(squares + 1e-06))


def make_right(own_rows, squares, columns):
    return pl.pallas_call(
        functools.partial(scale_kernel, columns),
        out_shape=jax.ShapeDtypeStruct(own_rows.shape, jnp.float32),
        compiler_params=pltpu.CompilerParams(vmem_limit_bytes=VMEM_LIMIT),
        name="scale",
    )(own_rows, squares)


def shards(momentum, gradient, right_in):
    row_count, col_count = momentum.shape[1:]
    rank = right_in.shape[1]
    replicas = lax.axis_size("replica")
    fsdp_count = lax.axis_size("fsdp")
    tensor_count = lax.axis_size("tensor")
    group_count = replicas * tensor_count
    band = row_count // group_count
    packed = 2 * (col_count // fsdp_count // replicas)
    slab = rank // tensor_count
    far = fsdp_count // NEAR
    near_groups = [[a * NEAR + b for b in range(NEAR)] for a in range(far)]
    far_groups = [[a * NEAR + b for a in range(far)] for b in range(NEAR)]

    def around(value, step):
        pairs = [(i, (i + step) % replicas) for i in range(replicas)]
        return lax.ppermute(value, "replica", pairs)

    *turned, right_copies, buffer = turn(momentum, gradient, right_in, replicas, fsdp_count)
    right_quarter = exchange(right_copies, "fsdp")
    parts = [turned[0]] + [around(turned[step], step) for step in range(1, replicas)]
    column_sum, partial_value = project(parts, right_quarter)

    partial_value = exchange(partial_value.reshape(group_count, band, rank), GROUP)
    projected = exchange(sum_copies(partial_value, 1.0 / replicas), GROUP).reshape(row_count, rank)

    terms = make_terms(column_sum, projected, fsdp_count, tensor_count)
    height = terms.shape[2]
    terms = exchange(terms.reshape(NEAR, far * height, LANES), "fsdp", near_groups)
    sums = exchange(sum_blocks(terms, far), "fsdp", far_groups)
    sums = exchange(sum_copies(sums, 1.0), "fsdp", far_groups).reshape(1, far * height, LANES)
    sums = exchange(jnp.broadcast_to(sums, (NEAR, far * height, LANES)), "fsdp", near_groups)
    sums = sums.reshape(NEAR, far, height, LANES)
    gram_matrix = exchange(take_slab(sums, packed, slab, tensor_count), "tensor").reshape(rank, rank)
    raw_quarter = take_raw(sums, packed)
    raw_parts = [raw_quarter] + [around(raw_quarter, -step) for step in range(1, replicas)]
    inverse, combined, left_factor, squares = make_factor(
        gram_matrix, projected, raw_quarter, replicas, row_count * fsdp_count, group_count
    )
    new_momentum, own_rows = update(buffer, combined, inverse, raw_parts)
    right_factor = make_right(own_rows, exchange(squares, GROUP), col_count * tensor_count)
    return (left_factor, right_factor, new_momentum)


def solution(mesh):
    placed = (
        P("replica", "fsdp", "tensor"),
        P("replica", "fsdp", "tensor"),
        P(("tensor", "fsdp"), None),
    )
    return jax.shard_map(
        shards,
        mesh=mesh,
        in_specs=placed,
        out_specs=(P("fsdp", None), P(("tensor", "fsdp"), None), P("replica", "fsdp", "tensor")),
        check_vma=False,
    )
```

```python
import functools
import math

import jax
import jax.numpy as jnp
from jax import lax
from jax.experimental import pallas as pl
from jax.experimental.pallas import tpu as pltpu
from jax.sharding import PartitionSpec as P

HIGHEST = lax.Precision.HIGHEST
GROUP = ("replica", "tensor")
PANEL = 64
NEAR = 4
LANES = 128
VMEM_LIMIT = 20 * 1024 * 1024
VMEM_WHOLE = 63 * 1024 * 1024


def exchange(blocks, axes, groups=None):
    return lax.all_to_all(blocks, axes, 0, 0, tiled=True, axis_index_groups=groups)


def pack(value):
    return jnp.concatenate([value[:, :LANES], value[:, LANES:]], axis=0)


def unpack(value):
    half = value.shape[0] // 2
    return jnp.concatenate([value[:half], value[half:]], axis=1)


def column_dot(left, right):
    return lax.dot_general(
        left, right, (((0,), (0,)), ((), ())), precision=HIGHEST, preferred_element_type=jnp.float32
    )


def row_dot(left, right):
    return lax.dot_general(
        left, right, (((1,), (1,)), ((), ())), precision=HIGHEST, preferred_element_type=jnp.float32
    )


def turn_kernel(momentum_ref, gradient_ref, right_ref, *refs):
    outs, (copies_ref, buffer_ref, sorted_rows) = refs[:-3], refs[-3:]
    replica = lax.axis_index("replica")
    buffer = momentum_ref[0] + gradient_ref[0].astype(jnp.float32)
    buffer_ref[0] = buffer
    turned = buffer.T
    replicas, blocks, packed = sorted_rows.shape[:3]
    piece = packed // 2
    for block in range(blocks):
        for part in range(replicas):
            start = (block * replicas + part) * piece
            rows = turned[start : start + piece, :]
            sorted_rows[part, block, :piece, :] = rows[:, :LANES]
            sorted_rows[part, block, piece:, :] = rows[:, LANES:]
    for step, out_ref in enumerate(outs):
        out_ref[...] = sorted_rows[lax.rem(replica + step, replicas)]

    @pl.when(pl.program_id(0) == 0)
    def _():
        rows = right_ref[:piece, :]
        for part in range(1, replicas):
            rows = jnp.where(replica == part, right_ref[part * piece : (part + 1) * piece, :], rows)
        copies_ref[...] = jnp.broadcast_to(pack(rows)[None], copies_ref.shape)


def turn(momentum, gradient, right_in, replicas, fsdp_count):
    row_count, col_count = momentum.shape[1:]
    own = col_count // fsdp_count
    group = math.lcm(own, LANES)
    steps = col_count // group
    packed = 2 * (own // replicas)
    block = (fsdp_count // steps, packed, LANES)
    whole = (fsdp_count, packed, LANES)
    columns = pl.BlockSpec((1, row_count, group), lambda i: (0, 0, i))
    return pl.pallas_call(
        turn_kernel,
        grid=(steps,),
        in_specs=[columns] * 2 + [pl.BlockSpec(right_in.shape, lambda i: (0, 0))],
        out_specs=[pl.BlockSpec(block, lambda i: (i, 0, 0))] * replicas
        + [pl.BlockSpec(whole, lambda i: (0, 0, 0)), columns],
        out_shape=[jax.ShapeDtypeStruct(whole, jnp.float32)] * (replicas + 1)
        + [jax.ShapeDtypeStruct(momentum.shape, jnp.float32)],
        scratch_shapes=[pltpu.VMEM((replicas,) + block, jnp.float32)],
        compiler_params=pltpu.CompilerParams(vmem_limit_bytes=VMEM_WHOLE),
        name="turn",
    )(momentum, gradient, right_in)


def project_kernel(part_refs, right_ref, sum_ref, out_ref, right):
    blocks, packed = right_ref.shape[:2]
    piece = packed // 2
    for block in range(blocks):
        total = part_refs[0][block]
        for part_ref in part_refs[1:]:
            total = total + part_ref[block]
        rows = slice(block * piece, (block + 1) * piece)
        sum_ref[rows, :] = unpack(total)
        right[rows, :] = unpack(right_ref[block])
    out_ref[...] = column_dot(sum_ref[...], right[...])


def project(parts, right_quarter):
    def body(*refs):
        project_kernel(refs[: len(parts)], *refs[len(parts) :])

    blocks, packed, _ = right_quarter.shape
    quarter, rank = blocks * packed // 2, 2 * LANES
    return pl.pallas_call(
        body,
        out_shape=[
            jax.ShapeDtypeStruct((quarter, 2 * LANES), jnp.float32),
            jax.ShapeDtypeStruct((2 * LANES, rank), jnp.float32),
        ],
        scratch_shapes=[pltpu.VMEM((quarter, rank), jnp.float32)],
        compiler_params=pltpu.CompilerParams(vmem_limit_bytes=VMEM_LIMIT),
        name="project",
    )(*parts, right_quarter)


def sum_copies_kernel(scale, blocks_ref, out_ref):
    total = jnp.sum(blocks_ref[...], axis=0, keepdims=True) * scale
    out_ref[...] = jnp.broadcast_to(total, out_ref.shape)


def sum_copies(blocks, scale):
    return pl.pallas_call(
        functools.partial(sum_copies_kernel, scale),
        out_shape=jax.ShapeDtypeStruct(blocks.shape, jnp.float32),
        compiler_params=pltpu.CompilerParams(vmem_limit_bytes=VMEM_LIMIT),
        name="sum_copies",
    )(blocks)


def sum_kernel(blocks_ref, out_ref):
    rows = out_ref.shape[1]
    for receiver in range(out_ref.shape[0]):
        part = slice(receiver * rows, (receiver + 1) * rows)
        total = blocks_ref[0, part, :]
        for sender in range(1, blocks_ref.shape[0]):
            total = total + blocks_ref[sender, part, :]
        out_ref[receiver] = total


def sum_blocks(blocks, receivers):
    rows = blocks.shape[1] // receivers
    return pl.pallas_call(
        sum_kernel,
        out_shape=jax.ShapeDtypeStruct((receivers, rows, LANES), jnp.float32),
        compiler_params=pltpu.CompilerParams(vmem_limit_bytes=VMEM_LIMIT),
        name="sum_blocks",
    )(blocks)


def terms_kernel(share, sum_ref, projected_ref, out_ref, gram):
    near, far, packed = out_ref.shape[:3]
    blocks = near * far
    piece = sum_ref.shape[0] // blocks
    slab = share * blocks
    projected = projected_ref[...]
    gram[...] = column_dot(projected, projected)
    rows = gram[pl.ds(pl.multiple_of(lax.axis_index("tensor") * slab, slab), slab), :]
    raw = jnp.dot(
        sum_ref[...], projected, precision=HIGHEST, preferred_element_type=jnp.float32
    )
    rest = jnp.zeros((packed - 2 * (piece + share), LANES), jnp.float32)
    for block in range(blocks):
        a, b = divmod(block, near)
        out_ref[b, a, : 2 * piece, :] = pack(raw[block * piece : (block + 1) * piece, :])
        tail = pack(rows[block * share : (block + 1) * share, :])
        out_ref[b, a, 2 * piece :, :] = jnp.concatenate([tail, rest], axis=0)


def make_terms(column_sum, projected, blocks, tensor_count):
    rank = projected.shape[1]
    share = rank // tensor_count // blocks
    packed = 2 * (column_sum.shape[0] // blocks + share)
    return pl.pallas_call(
        functools.partial(terms_kernel, share),
        out_shape=jax.ShapeDtypeStruct((NEAR, blocks // NEAR, -(-packed // 8) * 8, LANES), jnp.float32),
        scratch_shapes=[pltpu.VMEM((rank, rank), jnp.float32)],
        compiler_params=pltpu.CompilerParams(vmem_limit_bytes=VMEM_LIMIT),
        name="terms",
    )(column_sum, projected)


def slab_kernel(packed, sums_ref, slab_ref):
    near, far = sums_ref.shape[:2]
    share = slab_ref.shape[1] // (near * far)
    tail = slice(packed, packed + 2 * share)
    rows = [unpack(sums_ref[b, a, tail, :]) for a in range(far) for b in range(near)]
    slab_ref[...] = jnp.broadcast_to(jnp.concatenate(rows, axis=0)[None], slab_ref.shape)


def take_slab(sums, packed, slab, tensor_count):
    return pl.pallas_call(
        functools.partial(slab_kernel, packed),
        out_shape=jax.ShapeDtypeStruct((tensor_count, slab, 2 * LANES), jnp.float32),
        compiler_params=pltpu.CompilerParams(vmem_limit_bytes=VMEM_LIMIT),
        name="slab",
    )(sums)


def raw_kernel(sums_ref, raw_ref):
    near = sums_ref.shape[0]
    for block in range(raw_ref.shape[0]):
        a, b = divmod(block, near)
        raw_ref[block] = sums_ref[b, a, : raw_ref.shape[1], :]


def take_raw(sums, packed):
    near, far = sums.shape[:2]
    return pl.pallas_call(
        raw_kernel,
        out_shape=jax.ShapeDtypeStruct((near * far, packed, LANES), jnp.float32),
        compiler_params=pltpu.CompilerParams(vmem_limit_bytes=VMEM_LIMIT),
        name="raw",
    )(sums)


def invert_factor(work, inverse_ref):
    rank = work.shape[0]
    lane = lax.broadcasted_iota(jnp.int32, (PANEL, rank), 1)
    row = lax.broadcasted_iota(jnp.int32, (PANEL, rank), 0)
    lane8, row8 = lane[:8, :LANES], row[:8, :LANES]
    tiles = rank // LANES
    groups = PANEL // 8

    def every(value):
        return jnp.broadcast_to(value, (8, LANES))

    for panel in range(0, rank, PANEL):
        rows = [
            [
                work[panel + 8 * h : panel + 8 * h + 8, LANES * t : LANES * (t + 1)]
                for t in range(tiles)
            ]
            for h in range(groups)
        ]
        inverses = []
        for g in range(groups):
            tile, start = divmod(panel + 8 * g, LANES)
            shares = {
                h: [every(rows[h][tile][:, start + j : start + j + 1]) for j in range(8)]
                for h in range(g, groups)
            }
            pivot_rows = [[every(rows[g][t][j : j + 1]) for j in range(8)] for t in range(tiles)]
            pivot_inverses = None
            for k in range(8):
                inverse = 1.0 / every(shares[g][k][k : k + 1])
                if pivot_inverses is None:
                    pivot_inverses = inverse
                else:
                    pivot_inverses = jnp.where(row8 == k, inverse, pivot_inverses)
                pivot_row = [every(shares[g][j][k : k + 1]) for j in range(8)]
                for h in range(g, groups):
                    factor = shares[h][k] * inverse
                    if h == g:
                        factor = jnp.where(row8 > k, factor, 0.0)
                    for j in range(8):
                        if j != k:
                            shares[h][j] = shares[h][j] - factor * pivot_row[j]
                    shares[h][k] = jnp.where(row8 == k, 1.0, -factor) if h == g else -factor
            inverses.append(pivot_inverses)
            shares[g] = [jnp.where(row8 >= j, shares[g][j], 0.0) for j in range(8)]
            for h in range(groups - 1, g - 1, -1):
                for t in range(tiles):
                    products = [shares[h][j] * pivot_rows[t][j] for j in range(8)]
                    while len(products) > 1:
                        products = [a + b for a, b in zip(products[::2], products[1::2])]
                    total = products[0] if h == g else rows[h][t] + products[0]
                    if t == tile:
                        for j in range(8):
                            total = jnp.where(lane8 == start + j, shares[h][j], total)
                    rows[h][t] = total
        whole = jnp.concatenate([jnp.concatenate(r, axis=1) for r in rows], axis=0)
        scale = jnp.concatenate([jnp.concatenate([r] * tiles, axis=1) for r in inverses], axis=0)
        unit = jnp.where((lane > panel + row) & (lane < panel + PANEL), 0.0, whole)
        inverse_ref[panel : panel + PANEL, :] = jnp.where(lane <= panel + row, unit, 0.0) * jnp.sqrt(scale)
        below = panel + PANEL
        if below < rank:
            rest = work[below:, :]
            lanes = lax.broadcasted_iota(jnp.int32, rest.shape, 1)
            rest = jnp.where((lanes >= panel) & (lanes < below), 0.0, rest)
            first = below // LANES * LANES
            work[below:, :] = rest - column_dot((whole * scale)[:, first:], unit)[below - first :]


def factor_kernel(replicas, gram_ref, raw_ref, inverse_ref, squares_ref, work, raw):
    blocks, packed = raw_ref.shape[:2]
    piece = packed // 2
    for block in range(blocks):
        raw[block * piece : (block + 1) * piece, :] = unpack(raw_ref[block])
    work[...] = gram_ref[...]
    invert_factor(work, inverse_ref)
    inverse = inverse_ref[...] * (1.0 / replicas)
    inverse_ref[...] = inverse
    back = row_dot(raw[...], inverse)
    squares = pack(jnp.sum(back * back, axis=0, keepdims=True))
    rest = jnp.zeros((squares_ref.shape[1] - 2, LANES), jnp.float32)
    squares_ref[...] = jnp.broadcast_to(jnp.concatenate([squares, rest], axis=0)[None], squares_ref.shape)


def make_factor(gram_matrix, raw_quarter, replicas, group_count):
    rank = gram_matrix.shape[0]
    blocks, packed, _ = raw_quarter.shape
    return pl.pallas_call(
        functools.partial(factor_kernel, replicas),
        out_shape=[
            jax.ShapeDtypeStruct(gram_matrix.shape, jnp.float32),
            jax.ShapeDtypeStruct((group_count, 8, LANES), jnp.float32),
        ],
        scratch_shapes=[
            pltpu.VMEM(gram_matrix.shape, jnp.float32),
            pltpu.VMEM((blocks * packed // 2, rank), jnp.float32),
        ],
        compiler_params=pltpu.CompilerParams(vmem_limit_bytes=VMEM_LIMIT),
        cost_estimate=pl.CostEstimate(flops=3 * 10**10, bytes_accessed=10**6, transcendentals=0),
        name="factor",
    )(gram_matrix, raw_quarter)


def combine_kernel(replicas, rows, projected_ref, inverse_ref, left_ref, combined_ref):
    inverse = inverse_ref[...]
    ortho = row_dot(projected_ref[...], inverse) * replicas
    left_ref[...] = ortho * math.sqrt(rows)
    combined_ref[...] = jnp.dot(
        ortho, inverse, precision=HIGHEST, preferred_element_type=jnp.float32
    )


def combine(projected, inverse, replicas, rows):
    return pl.pallas_call(
        functools.partial(combine_kernel, replicas, rows),
        out_shape=[jax.ShapeDtypeStruct(projected.shape, jnp.float32)] * 2,
        compiler_params=pltpu.CompilerParams(vmem_limit_bytes=VMEM_LIMIT),
        name="combine",
    )(projected, inverse)


def update_kernel(buffer_ref, ortho_ref, inverse_ref, *refs):
    parts, (out_ref, own_ref, sorted_rows, raw) = refs[:-4], refs[-4:]
    replicas, blocks, packed = sorted_rows.shape[:3]
    piece = packed // 2
    own = replicas * piece
    place, own_block = lax.axis_index("replica"), lax.axis_index("fsdp")
    for step, part_ref in enumerate(parts):
        sorted_rows[lax.rem(place + step, replicas)] = part_ref[...]
    for block in range(blocks):
        for replica in range(replicas):
            start = block * own + replica * piece
            raw[start : start + piece, :] = unpack(sorted_rows[replica, block])
    correction = row_dot(ortho_ref[...], raw[...])
    out_ref[0] = buffer_ref[0] - 0.1 * correction

    @pl.when(own_block // blocks == pl.program_id(0))
    def _():
        start = pl.multiple_of(lax.rem(own_block, blocks) * own, 8)
        own_ref[...] = row_dot(raw[pl.ds(start, own), :], inverse_ref[...])


def update(buffer, orthonormal, inverse, parts):
    row_count, own_count = buffer.shape[1:]
    replicas = len(parts)
    fsdp_count, packed, _ = parts[0].shape
    rank = orthonormal.shape[1]
    own = own_count // fsdp_count
    group = math.lcm(own, LANES)
    steps = own_count // group
    columns = pl.BlockSpec((1, row_count, group), lambda i: (0, 0, i))
    block = (fsdp_count // steps, packed, LANES)
    return pl.pallas_call(
        update_kernel,
        grid=(steps,),
        in_specs=[
            columns,
            pl.BlockSpec((row_count, rank), lambda i: (0, 0)),
            pl.BlockSpec((rank, rank), lambda i: (0, 0)),
        ]
        + [pl.BlockSpec(block, lambda i: (i, 0, 0))] * replicas,
        out_specs=[columns, pl.BlockSpec((own, rank), lambda i: (0, 0))],
        out_shape=[
            jax.ShapeDtypeStruct(buffer.shape, jnp.float32),
            jax.ShapeDtypeStruct((own, rank), jnp.float32),
        ],
        scratch_shapes=[
            pltpu.VMEM((replicas,) + block, jnp.float32),
            pltpu.VMEM((group, rank), jnp.float32),
        ],
        compiler_params=pltpu.CompilerParams(vmem_limit_bytes=VMEM_LIMIT),
        input_output_aliases={0: 0},
        name="update",
    )(buffer, orthonormal, inverse, *parts)


def scale_kernel(columns, own_ref, squares_ref, out_ref):
    squares = unpack(jnp.sum(squares_ref[...], axis=0)[:2])
    out_ref[...] = own_ref[...] * (math.sqrt(columns) / jnp.sqrt(squares + 1e-06))


def make_right(own_rows, squares, columns):
    return pl.pallas_call(
        functools.partial(scale_kernel, columns),
        out_shape=jax.ShapeDtypeStruct(own_rows.shape, jnp.float32),
        compiler_params=pltpu.CompilerParams(vmem_limit_bytes=VMEM_LIMIT),
        name="scale",
    )(own_rows, squares)


def shards(momentum, gradient, right_in):
    row_count, col_count = momentum.shape[1:]
    rank = right_in.shape[1]
    replicas = lax.axis_size("replica")
    fsdp_count = lax.axis_size("fsdp")
    tensor_count = lax.axis_size("tensor")
    group_count = replicas * tensor_count
    band = row_count // group_count
    packed = 2 * (col_count // fsdp_count // replicas)
    slab = rank // tensor_count
    far = fsdp_count // NEAR
    near_groups = [[a * NEAR + b for b in range(NEAR)] for a in range(far)]
    far_groups = [[a * NEAR + b for a in range(far)] for b in range(NEAR)]

    def around(value, step):
        pairs = [(i, (i + step) % replicas) for i in range(replicas)]
        return lax.ppermute(value, "replica", pairs)

    *turned, right_copies, buffer = turn(momentum, gradient, right_in, replicas, fsdp_count)
    right_quarter = exchange(right_copies, "fsdp")
    parts = [turned[0]] + [around(turned[step], step) for step in range(1, replicas)]
    column_sum, partial_value = project(parts, right_quarter)

    partial_value = exchange(partial_value.reshape(group_count, band, rank), GROUP)
    projected = exchange(sum_copies(partial_value, 1.0 / replicas), GROUP).reshape(row_count, rank)

    terms = make_terms(column_sum, projected, fsdp_count, tensor_count)
    height = terms.shape[2]
    terms = exchange(terms.reshape(NEAR, far * height, LANES), "fsdp", near_groups)
    sums = exchange(sum_blocks(terms, far), "fsdp", far_groups)
    sums = exchange(sum_copies(sums, 1.0), "fsdp", far_groups).reshape(1, far * height, LANES)
    sums = exchange(jnp.broadcast_to(sums, (NEAR, far * height, LANES)), "fsdp", near_groups)
    sums = sums.reshape(NEAR, far, height, LANES)
    gram_matrix = exchange(take_slab(sums, packed, slab, tensor_count), "tensor").reshape(rank, rank)
    raw_quarter = take_raw(sums, packed)
    raw_parts = [raw_quarter] + [around(raw_quarter, -step) for step in range(1, replicas)]
    inverse, squares = make_factor(gram_matrix, raw_quarter, replicas, group_count)
    left_factor, combined = combine(projected, inverse, replicas, row_count * fsdp_count)
    new_momentum, own_rows = update(buffer, combined, inverse, raw_parts)
    right_factor = make_right(own_rows, exchange(squares, GROUP), col_count * tensor_count)
    return (left_factor, right_factor, new_momentum)


def solution(mesh):
    placed = (
        P("replica", "fsdp", "tensor"),
        P("replica", "fsdp", "tensor"),
        P(("tensor", "fsdp"), None),
    )
    return jax.shard_map(
        shards,
        mesh=mesh,
        in_specs=placed,
        out_specs=(P("fsdp", None), P(("tensor", "fsdp"), None), P("replica", "fsdp", "tensor")),
        check_vma=False,
    )
```

```python
import functools
import math

import jax
import jax.numpy as jnp
from jax import lax
from jax.experimental import pallas as pl
from jax.experimental.pallas import tpu as pltpu
from jax.sharding import PartitionSpec as P

HIGHEST = lax.Precision.HIGHEST
GROUP = ("replica", "tensor")
PANEL = 64
NEAR = 4
LANES = 128
VMEM_LIMIT = 20 * 1024 * 1024
VMEM_WHOLE = 63 * 1024 * 1024


def exchange(blocks, axes, groups=None):
    return lax.all_to_all(blocks, axes, 0, 0, tiled=True, axis_index_groups=groups)


def pack(value):
    return jnp.concatenate([value[:, :LANES], value[:, LANES:]], axis=0)


def unpack(value):
    half = value.shape[0] // 2
    return jnp.concatenate([value[:half], value[half:]], axis=1)


def column_dot(left, right):
    return lax.dot_general(
        left, right, (((0,), (0,)), ((), ())), precision=HIGHEST, preferred_element_type=jnp.float32
    )


def row_dot(left, right):
    return lax.dot_general(
        left, right, (((1,), (1,)), ((), ())), precision=HIGHEST, preferred_element_type=jnp.float32
    )


def turn_kernel(momentum_ref, gradient_ref, right_ref, *refs):
    outs, (copies_ref, buffer_ref, sorted_rows) = refs[:-3], refs[-3:]
    replica = lax.axis_index("replica")
    buffer = momentum_ref[0] + gradient_ref[0].astype(jnp.float32)
    buffer_ref[0] = buffer
    turned = buffer.T
    replicas, blocks, packed = sorted_rows.shape[:3]
    piece = packed // 2
    for block in range(blocks):
        for part in range(replicas):
            start = (block * replicas + part) * piece
            rows = turned[start : start + piece, :]
            sorted_rows[part, block, :piece, :] = rows[:, :LANES]
            sorted_rows[part, block, piece:, :] = rows[:, LANES:]
    for step, out_ref in enumerate(outs):
        out_ref[...] = sorted_rows[lax.rem(replica + step, replicas)]

    @pl.when(pl.program_id(0) == 0)
    def _():
        rows = right_ref[:piece, :]
        for part in range(1, replicas):
            rows = jnp.where(replica == part, right_ref[part * piece : (part + 1) * piece, :], rows)
        copies_ref[...] = jnp.broadcast_to(pack(rows)[None], copies_ref.shape)


def turn(momentum, gradient, right_in, replicas, fsdp_count):
    row_count, col_count = momentum.shape[1:]
    own = col_count // fsdp_count
    group = math.lcm(own, LANES)
    steps = col_count // group
    packed = 2 * (own // replicas)
    block = (fsdp_count // steps, packed, LANES)
    whole = (fsdp_count, packed, LANES)
    columns = pl.BlockSpec((1, row_count, group), lambda i: (0, 0, i))
    return pl.pallas_call(
        turn_kernel,
        grid=(steps,),
        in_specs=[columns] * 2 + [pl.BlockSpec(right_in.shape, lambda i: (0, 0))],
        out_specs=[pl.BlockSpec(block, lambda i: (i, 0, 0))] * replicas
        + [pl.BlockSpec(whole, lambda i: (0, 0, 0)), columns],
        out_shape=[jax.ShapeDtypeStruct(whole, jnp.float32)] * (replicas + 1)
        + [jax.ShapeDtypeStruct(momentum.shape, jnp.float32)],
        scratch_shapes=[pltpu.VMEM((replicas,) + block, jnp.float32)],
        compiler_params=pltpu.CompilerParams(vmem_limit_bytes=VMEM_WHOLE),
        name="turn",
    )(momentum, gradient, right_in)


def own_kernel(part_ref, out_ref):
    blocks, packed = part_ref.shape[:2]
    piece = packed // 2
    for block in range(blocks):
        out_ref[block * piece : (block + 1) * piece, :] = unpack(part_ref[block])


def unpack_own(part):
    blocks, packed, _ = part.shape
    return pl.pallas_call(
        own_kernel,
        out_shape=jax.ShapeDtypeStruct((blocks * packed // 2, 2 * LANES), jnp.float32),
        compiler_params=pltpu.CompilerParams(vmem_limit_bytes=VMEM_LIMIT),
        cost_estimate=pl.CostEstimate(flops=10**9, bytes_accessed=10**6, transcendentals=0),
        name="own",
    )(part)


def project_kernel(part_refs, right_ref, sum_ref, out_ref, right):
    blocks, packed = right_ref.shape[:2]
    piece = packed // 2
    for block in range(blocks):
        rows = slice(block * piece, (block + 1) * piece)
        total = part_refs[0][rows, :]
        for part_ref in part_refs[1:]:
            total = total + unpack(part_ref[block])
        sum_ref[rows, :] = total
        right[rows, :] = unpack(right_ref[block])
    out_ref[...] = column_dot(sum_ref[...], right[...])


def project(parts, right_quarter):
    def body(*refs):
        project_kernel(refs[: len(parts)], *refs[len(parts) :])

    blocks, packed, _ = right_quarter.shape
    quarter, rank = blocks * packed // 2, 2 * LANES
    return pl.pallas_call(
        body,
        out_shape=[
            jax.ShapeDtypeStruct((quarter, 2 * LANES), jnp.float32),
            jax.ShapeDtypeStruct((2 * LANES, rank), jnp.float32),
        ],
        scratch_shapes=[pltpu.VMEM((quarter, rank), jnp.float32)],
        compiler_params=pltpu.CompilerParams(vmem_limit_bytes=VMEM_LIMIT),
        name="project",
    )(*parts, right_quarter)


def sum_copies_kernel(scale, blocks_ref, out_ref):
    total = jnp.sum(blocks_ref[...], axis=0, keepdims=True) * scale
    out_ref[...] = jnp.broadcast_to(total, out_ref.shape)


def sum_copies(blocks, scale):
    return pl.pallas_call(
        functools.partial(sum_copies_kernel, scale),
        out_shape=jax.ShapeDtypeStruct(blocks.shape, jnp.float32),
        compiler_params=pltpu.CompilerParams(vmem_limit_bytes=VMEM_LIMIT),
        name="sum_copies",
    )(blocks)


def sum_kernel(blocks_ref, out_ref):
    rows = out_ref.shape[1]
    for receiver in range(out_ref.shape[0]):
        part = slice(receiver * rows, (receiver + 1) * rows)
        total = blocks_ref[0, part, :]
        for sender in range(1, blocks_ref.shape[0]):
            total = total + blocks_ref[sender, part, :]
        out_ref[receiver] = total


def sum_blocks(blocks, receivers):
    rows = blocks.shape[1] // receivers
    return pl.pallas_call(
        sum_kernel,
        out_shape=jax.ShapeDtypeStruct((receivers, rows, LANES), jnp.float32),
        compiler_params=pltpu.CompilerParams(vmem_limit_bytes=VMEM_LIMIT),
        name="sum_blocks",
    )(blocks)


def terms_kernel(share, sum_ref, projected_ref, out_ref, gram):
    near, far, packed = out_ref.shape[:3]
    blocks = near * far
    piece = sum_ref.shape[0] // blocks
    slab = share * blocks
    projected = projected_ref[...]
    gram[...] = column_dot(projected, projected)
    rows = gram[pl.ds(pl.multiple_of(lax.axis_index("tensor") * slab, slab), slab), :]
    raw = jnp.dot(
        sum_ref[...], projected, precision=HIGHEST, preferred_element_type=jnp.float32
    )
    rest = jnp.zeros((packed - 2 * (piece + share), LANES), jnp.float32)
    for block in range(blocks):
        a, b = divmod(block, near)
        out_ref[b, a, : 2 * piece, :] = pack(raw[block * piece : (block + 1) * piece, :])
        tail = pack(rows[block * share : (block + 1) * share, :])
        out_ref[b, a, 2 * piece :, :] = jnp.concatenate([tail, rest], axis=0)


def make_terms(column_sum, projected, blocks, tensor_count):
    rank = projected.shape[1]
    share = rank // tensor_count // blocks
    packed = 2 * (column_sum.shape[0] // blocks + share)
    return pl.pallas_call(
        functools.partial(terms_kernel, share),
        out_shape=jax.ShapeDtypeStruct((NEAR, blocks // NEAR, -(-packed // 8) * 8, LANES), jnp.float32),
        scratch_shapes=[pltpu.VMEM((rank, rank), jnp.float32)],
        compiler_params=pltpu.CompilerParams(vmem_limit_bytes=VMEM_LIMIT),
        name="terms",
    )(column_sum, projected)


def slab_kernel(packed, sums_ref, slab_ref):
    near, far = sums_ref.shape[:2]
    share = slab_ref.shape[1] // (near * far)
    tail = slice(packed, packed + 2 * share)
    rows = [unpack(sums_ref[b, a, tail, :]) for a in range(far) for b in range(near)]
    slab_ref[...] = jnp.broadcast_to(jnp.concatenate(rows, axis=0)[None], slab_ref.shape)


def take_slab(sums, packed, slab, tensor_count):
    return pl.pallas_call(
        functools.partial(slab_kernel, packed),
        out_shape=jax.ShapeDtypeStruct((tensor_count, slab, 2 * LANES), jnp.float32),
        compiler_params=pltpu.CompilerParams(vmem_limit_bytes=VMEM_LIMIT),
        name="slab",
    )(sums)


def raw_kernel(sums_ref, raw_ref):
    near = sums_ref.shape[0]
    for block in range(raw_ref.shape[0]):
        a, b = divmod(block, near)
        raw_ref[block] = sums_ref[b, a, : raw_ref.shape[1], :]


def take_raw(sums, packed):
    near, far = sums.shape[:2]
    return pl.pallas_call(
        raw_kernel,
        out_shape=jax.ShapeDtypeStruct((near * far, packed, LANES), jnp.float32),
        compiler_params=pltpu.CompilerParams(vmem_limit_bytes=VMEM_LIMIT),
        name="raw",
    )(sums)


def invert_factor(work, inverse_ref):
    rank = work.shape[0]
    lane = lax.broadcasted_iota(jnp.int32, (PANEL, rank), 1)
    row = lax.broadcasted_iota(jnp.int32, (PANEL, rank), 0)
    lane8, row8 = lane[:8, :LANES], row[:8, :LANES]
    tiles = rank // LANES
    groups = PANEL // 8

    def every(value):
        return jnp.broadcast_to(value, (8, LANES))

    for panel in range(0, rank, PANEL):
        rows = [
            [
                work[panel + 8 * h : panel + 8 * h + 8, LANES * t : LANES * (t + 1)]
                for t in range(tiles)
            ]
            for h in range(groups)
        ]
        inverses = []
        for g in range(groups):
            tile, start = divmod(panel + 8 * g, LANES)
            shares = {
                h: [every(rows[h][tile][:, start + j : start + j + 1]) for j in range(8)]
                for h in range(g, groups)
            }
            pivot_rows = [[every(rows[g][t][j : j + 1]) for j in range(8)] for t in range(tiles)]
            pivot_inverses = None
            for k in range(8):
                inverse = 1.0 / every(shares[g][k][k : k + 1])
                if pivot_inverses is None:
                    pivot_inverses = inverse
                else:
                    pivot_inverses = jnp.where(row8 == k, inverse, pivot_inverses)
                pivot_row = [every(shares[g][j][k : k + 1]) for j in range(8)]
                for h in range(g, groups):
                    factor = shares[h][k] * inverse
                    if h == g:
                        factor = jnp.where(row8 > k, factor, 0.0)
                    for j in range(8):
                        if j != k:
                            shares[h][j] = shares[h][j] - factor * pivot_row[j]
                    shares[h][k] = jnp.where(row8 == k, 1.0, -factor) if h == g else -factor
            inverses.append(pivot_inverses)
            shares[g] = [jnp.where(row8 >= j, shares[g][j], 0.0) for j in range(8)]
            for h in range(groups - 1, g - 1, -1):
                for t in range(tiles):
                    products = [shares[h][j] * pivot_rows[t][j] for j in range(8)]
                    while len(products) > 1:
                        products = [a + b for a, b in zip(products[::2], products[1::2])]
                    total = products[0] if h == g else rows[h][t] + products[0]
                    if t == tile:
                        for j in range(8):
                            total = jnp.where(lane8 == start + j, shares[h][j], total)
                    rows[h][t] = total
        whole = jnp.concatenate([jnp.concatenate(r, axis=1) for r in rows], axis=0)
        scale = jnp.concatenate([jnp.concatenate([r] * tiles, axis=1) for r in inverses], axis=0)
        unit = jnp.where((lane > panel + row) & (lane < panel + PANEL), 0.0, whole)
        inverse_ref[panel : panel + PANEL, :] = jnp.where(lane <= panel + row, unit, 0.0) * jnp.sqrt(scale)
        below = panel + PANEL
        if below < rank:
            rest = work[below:, :]
            lanes = lax.broadcasted_iota(jnp.int32, rest.shape, 1)
            rest = jnp.where((lanes >= panel) & (lanes < below), 0.0, rest)
            first = below // LANES * LANES
            work[below:, :] = rest - column_dot((whole * scale)[:, first:], unit)[below - first :]


def factor_kernel(replicas, gram_ref, raw_ref, inverse_ref, squares_ref, work, raw):
    blocks, packed = raw_ref.shape[:2]
    piece = packed // 2
    for block in range(blocks):
        raw[block * piece : (block + 1) * piece, :] = unpack(raw_ref[block])
    work[...] = gram_ref[...]
    invert_factor(work, inverse_ref)
    inverse = inverse_ref[...] * (1.0 / replicas)
    inverse_ref[...] = inverse
    back = row_dot(raw[...], inverse)
    squares = pack(jnp.sum(back * back, axis=0, keepdims=True))
    rest = jnp.zeros((squares_ref.shape[1] - 2, LANES), jnp.float32)
    squares_ref[...] = jnp.broadcast_to(jnp.concatenate([squares, rest], axis=0)[None], squares_ref.shape)


def make_factor(gram_matrix, raw_quarter, replicas, group_count):
    rank = gram_matrix.shape[0]
    blocks, packed, _ = raw_quarter.shape
    return pl.pallas_call(
        functools.partial(factor_kernel, replicas),
        out_shape=[
            jax.ShapeDtypeStruct(gram_matrix.shape, jnp.float32),
            jax.ShapeDtypeStruct((group_count, 8, LANES), jnp.float32),
        ],
        scratch_shapes=[
            pltpu.VMEM(gram_matrix.shape, jnp.float32),
            pltpu.VMEM((blocks * packed // 2, rank), jnp.float32),
        ],
        compiler_params=pltpu.CompilerParams(vmem_limit_bytes=VMEM_LIMIT),
        cost_estimate=pl.CostEstimate(flops=3 * 10**10, bytes_accessed=10**6, transcendentals=0),
        name="factor",
    )(gram_matrix, raw_quarter)


def combine_kernel(replicas, rows, projected_ref, inverse_ref, left_ref, combined_ref):
    inverse = inverse_ref[...]
    ortho = row_dot(projected_ref[...], inverse) * replicas
    left_ref[...] = ortho * math.sqrt(rows)
    combined_ref[...] = jnp.dot(
        ortho, inverse, precision=HIGHEST, preferred_element_type=jnp.float32
    )


def combine(projected, inverse, replicas, rows):
    return pl.pallas_call(
        functools.partial(combine_kernel, replicas, rows),
        out_shape=[jax.ShapeDtypeStruct(projected.shape, jnp.float32)] * 2,
        compiler_params=pltpu.CompilerParams(vmem_limit_bytes=VMEM_LIMIT),
        name="combine",
    )(projected, inverse)


def update_kernel(buffer_ref, ortho_ref, inverse_ref, *refs):
    parts, (out_ref, own_ref, sorted_rows, raw) = refs[:-4], refs[-4:]
    replicas, blocks, packed = sorted_rows.shape[:3]
    piece = packed // 2
    own = replicas * piece
    place, own_block = lax.axis_index("replica"), lax.axis_index("fsdp")
    for step, part_ref in enumerate(parts):
        sorted_rows[lax.rem(place + step, replicas)] = part_ref[...]
    for block in range(blocks):
        for replica in range(replicas):
            start = block * own + replica * piece
            raw[start : start + piece, :] = unpack(sorted_rows[replica, block])
    correction = row_dot(ortho_ref[...], raw[...])
    out_ref[0] = buffer_ref[0] - 0.1 * correction

    @pl.when(own_block // blocks == pl.program_id(0))
    def _():
        start = pl.multiple_of(lax.rem(own_block, blocks) * own, 8)
        own_ref[...] = row_dot(raw[pl.ds(start, own), :], inverse_ref[...])


def update(buffer, orthonormal, inverse, parts):
    row_count, own_count = buffer.shape[1:]
    replicas = len(parts)
    fsdp_count, packed, _ = parts[0].shape
    rank = orthonormal.shape[1]
    own = own_count // fsdp_count
    group = math.lcm(own, LANES)
    steps = own_count // group
    columns = pl.BlockSpec((1, row_count, group), lambda i: (0, 0, i))
    block = (fsdp_count // steps, packed, LANES)
    return pl.pallas_call(
        update_kernel,
        grid=(steps,),
        in_specs=[
            columns,
            pl.BlockSpec((row_count, rank), lambda i: (0, 0)),
            pl.BlockSpec((rank, rank), lambda i: (0, 0)),
        ]
        + [pl.BlockSpec(block, lambda i: (i, 0, 0))] * replicas,
        out_specs=[columns, pl.BlockSpec((own, rank), lambda i: (0, 0))],
        out_shape=[
            jax.ShapeDtypeStruct(buffer.shape, jnp.float32),
            jax.ShapeDtypeStruct((own, rank), jnp.float32),
        ],
        scratch_shapes=[
            pltpu.VMEM((replicas,) + block, jnp.float32),
            pltpu.VMEM((group, rank), jnp.float32),
        ],
        compiler_params=pltpu.CompilerParams(vmem_limit_bytes=VMEM_LIMIT),
        input_output_aliases={0: 0},
        name="update",
    )(buffer, orthonormal, inverse, *parts)


def scale_kernel(columns, own_ref, squares_ref, out_ref):
    squares = unpack(jnp.sum(squares_ref[...], axis=0)[:2])
    out_ref[...] = own_ref[...] * (math.sqrt(columns) / jnp.sqrt(squares + 1e-06))


def make_right(own_rows, squares, columns):
    return pl.pallas_call(
        functools.partial(scale_kernel, columns),
        out_shape=jax.ShapeDtypeStruct(own_rows.shape, jnp.float32),
        compiler_params=pltpu.CompilerParams(vmem_limit_bytes=VMEM_LIMIT),
        name="scale",
    )(own_rows, squares)


def shards(momentum, gradient, right_in):
    row_count, col_count = momentum.shape[1:]
    rank = right_in.shape[1]
    replicas = lax.axis_size("replica")
    fsdp_count = lax.axis_size("fsdp")
    tensor_count = lax.axis_size("tensor")
    group_count = replicas * tensor_count
    band = row_count // group_count
    packed = 2 * (col_count // fsdp_count // replicas)
    slab = rank // tensor_count
    far = fsdp_count // NEAR
    near_groups = [[a * NEAR + b for b in range(NEAR)] for a in range(far)]
    far_groups = [[a * NEAR + b for a in range(far)] for b in range(NEAR)]

    def around(value, step):
        pairs = [(i, (i + step) % replicas) for i in range(replicas)]
        return lax.ppermute(value, "replica", pairs)

    *turned, right_copies, buffer = turn(momentum, gradient, right_in, replicas, fsdp_count)
    right_quarter = exchange(right_copies, "fsdp")
    parts = [unpack_own(turned[0])] + [around(turned[step], step) for step in range(1, replicas)]
    column_sum, partial_value = project(parts, right_quarter)

    partial_value = exchange(partial_value.reshape(group_count, band, rank), GROUP)
    projected = exchange(sum_copies(partial_value, 1.0 / replicas), GROUP).reshape(row_count, rank)

    terms = make_terms(column_sum, projected, fsdp_count, tensor_count)
    height = terms.shape[2]
    terms = exchange(terms.reshape(NEAR, far * height, LANES), "fsdp", near_groups)
    sums = exchange(sum_blocks(terms, far), "fsdp", far_groups)
    sums = exchange(sum_copies(sums, 1.0), "fsdp", far_groups).reshape(1, far * height, LANES)
    sums = exchange(jnp.broadcast_to(sums, (NEAR, far * height, LANES)), "fsdp", near_groups)
    sums = sums.reshape(NEAR, far, height, LANES)
    gram_matrix = exchange(take_slab(sums, packed, slab, tensor_count), "tensor").reshape(rank, rank)
    raw_quarter = take_raw(sums, packed)
    raw_parts = [raw_quarter] + [around(raw_quarter, -step) for step in range(1, replicas)]
    inverse, squares = make_factor(gram_matrix, raw_quarter, replicas, group_count)
    left_factor, combined = combine(projected, inverse, replicas, row_count * fsdp_count)
    new_momentum, own_rows = update(buffer, combined, inverse, raw_parts)
    right_factor = make_right(own_rows, exchange(squares, GROUP), col_count * tensor_count)
    return (left_factor, right_factor, new_momentum)


def solution(mesh):
    placed = (
        P("replica", "fsdp", "tensor"),
        P("replica", "fsdp", "tensor"),
        P(("tensor", "fsdp"), None),
    )
    return jax.shard_map(
        shards,
        mesh=mesh,
        in_specs=placed,
        out_specs=(P("fsdp", None), P(("tensor", "fsdp"), None), P("replica", "fsdp", "tensor")),
        check_vma=False,
    )
```
